256 devices in a mesh: slot: 16 (over z, core), hid: 16 (over y, x).
Axes of the slice: x: 4, y: 4, z: 8, core: 2. Of those that a mesh axis runs over, the one named last changes fastest.
Arguments:
- cotangent: bfloat16 [32768, 2048], P('slot', 'hid'), may hold values from -6 to 6
- hidden: bfloat16 [32768, 8192], P('slot', 'hid'), may hold values from -6 to 6
- weights: bfloat16 [16, 8192, 2048], P('slot', 'hid'), may hold values from -0.125 to 0.125
- slot_experts: int32 [16, 1], replicated, may hold values from 0 to 3
- next_experts: int32 [16, 1], replicated, may hold values from 0 to 3
- row_counts: int32 [16], replicated, may hold values from 1 to 2048, 20480 in all
- master: float32 [4, 8192, 2048], P(None, 'hid', 'slot'), may hold values from -3 to 3
- momentum: float32 [4, 8192, 2048], P(None, 'hid', 'slot'), may hold values from -96 to 96
Outputs:
- input_grad: bfloat16 [32768, 8192], P('slot', 'hid')
- new_momentum: float32 [4, 8192, 2048], P(None, 'hid', 'slot')
- new_master: float32 [4, 8192, 2048], P(None, 'hid', 'slot')
- placed: bfloat16 [16, 8192, 2048], P('slot', 'hid')
The draws below stay inside these ranges and needn't reach their ends.
Inputs may be any that keep to these rules, and one draw needn't show every extreme that they name: `slot_experts`: every expert 0 to 3 is held by at least one slot. `next_experts`: every expert 0 to 3 is held by at least one slot. `row_counts`: the counts sum to 20480.
All inputs are finite; a program needn't handle non-finite values.
Results may differ from the reference program's by a relative error of at most 0.015.
Values may be sent and summed in bfloat16 or wider, within the bound.
No kernel may reach another device: no remote copies, remote signals or barrier semaphores. Data moves between devices by JAX's collectives and lax.ppermute only.
A program may use at most 128 MiB of HBM per device.

```python
import math
import jax
import jax.numpy as jnp
import numpy as np
from jax import lax

D = 2048
FF = 8192
ROWS = 2048
NE = 4
SLOTS = 16


def block_scale(rng, extent, cuts, smallest, top_value):
    def one(position, parts):
        draws = jax.random.uniform(jax.random.fold_in(jax.random.fold_in(rng, 6), position), (parts,), jnp.float32, smallest / len(cuts), top_value / len(cuts))
        return jnp.repeat(jnp.exp(draws), extent[position] // parts).reshape((-1,) + (1,) * (len(extent) - position - 1))

    level = one(*cuts[0])
    for cut in cuts[1:]:
        level = level * one(*cut)
    return level


def picks_of(own_key, rows, amount, top, lift):
    order = jax.random.permutation(jax.random.fold_in(own_key, 1), amount)
    boost = order
    for power in range(3):
        boost = boost * boost // amount
    boost = boost * lift // amount
    chance = jax.random.randint(jax.random.fold_in(own_key, 2), (rows, amount), 0, 4096) + boost
    sure = jax.random.permutation(jax.random.fold_in(own_key, 3), rows)[jnp.arange(amount) % rows]
    chance = jnp.where(jnp.arange(rows)[:, None] == sure[None, :], 1 << 14, chance)
    priority = chance * amount + jnp.arange(amount)
    return lax.top_k(priority.astype(jnp.int32), top)[1].astype(jnp.int32)


def split_up(number_of, total, limit, lean):
    portions = [(1 << 20) // math.isqrt(grade ** lean) + 1 for grade in range(2, number_of + 1)]
    spare, holding = total - limit - (number_of - 1), [1] * (number_of - 1)
    while spare > 0:
        free = [i for i in range(number_of - 1) if holding[i] < limit]
        mass, remaining = sum([portions[i] for i in free]), spare
        for i in free:
            more = min(limit - holding[i], max(1, remaining * portions[i] // mass), spare)
            holding[i] = holding[i] + more
            spare = spare - more
    return np.array([limit] + holding)


def uneven(stream_key, count, total, most, slope):
    if count == 2:
        one = jax.random.randint(stream_key, (), max(1, total - most), min(most, total - 1) + 1)
        return jnp.stack([one, total - one])
    lengths = jnp.asarray(split_up(count, total, most, slope), jnp.int32)
    twos = (count - 1) // 2
    source_of, sink = lengths[1:1 + 2 * twos:2], lengths[2:2 + 2 * twos:2]
    margin = jnp.minimum(source_of - 1, most - sink)
    moved = jax.random.randint(jax.random.fold_in(stream_key, 1), (twos,), 0, 1 << 20) % (margin + 1)
    lengths = lengths.at[1:1 + 2 * twos:2].set(source_of - moved).at[2:2 + 2 * twos:2].set(sink + moved)
    return lengths[jax.random.permutation(jax.random.fold_in(stream_key, 2), count)]


def centred(stream_key, shape, scale, bound, cuts=(), held_as=jnp.bfloat16):
    loudness = block_scale(stream_key, shape, cuts, -0.22, 0.18) if cuts else 1.0
    result = jax.random.normal(stream_key, shape, jnp.float32) * scale * loudness
    return jnp.minimum(jnp.maximum(result, -bound), bound).astype(held_as)


def setup_inputs(seed: int = 0) -> dict:
    keys = jax.random.split(jax.random.key(seed), 9)
    return {
        "cotangent": centred(keys[0], (SLOTS * ROWS, D), 1.0, 6.0, ((0, 16), (1, 16))),
        "hidden": centred(keys[1], (SLOTS * ROWS, FF), 1.0, 6.0, ((0, 16), (1, 16))),
        "weights": centred(keys[2], (SLOTS, FF, D), D ** -0.5, 0.125, ((0, 16), (1, 16))),
        "slot_experts": picks_of(keys[3], SLOTS, NE, 1, 4096),
        "next_experts": picks_of(keys[4], SLOTS, NE, 1, 2048),
        "row_counts": uneven(keys[5], SLOTS, SLOTS * ROWS * 5 // 8, ROWS, 2).astype(jnp.int32),
        "master": centred(keys[6], (NE, FF, D), 0.5, 3.0, ((1, 16), (2, 16)), jnp.float32),
        "momentum": centred(keys[7], (NE, FF, D), 16.0, 96.0, ((1, 16), (2, 16)), jnp.float32),
    }


momentum_decay = 0.9
learn_rate = 0.01


def reference(cotangent, hidden, weights, slot_experts, next_experts, row_counts, master, momentum):
    slot_count = weights.shape[0]
    row_span = cotangent.shape[0] // slot_count
    live_mask = (jnp.arange(row_span, dtype=jnp.int32)[None, :] < row_counts[:, None]).astype(cotangent.dtype)
    masked = cotangent.reshape(slot_count, row_span, -1) * live_mask[:, :, None]
    hid_rows = hidden.reshape(slot_count, row_span, -1)

    def per_slot(totals, inputs):
        grad_rows, act_rows, weight_rows, expert = inputs
        hid_grad = jnp.dot(grad_rows, weight_rows.T, preferred_element_type=jnp.float32).astype(jnp.bfloat16)
        w_grad = jnp.dot(act_rows.T, grad_rows, preferred_element_type=jnp.float32)
        select = (jnp.arange(NE, dtype=jnp.int32) == expert[0]).astype(jnp.float32)
        return totals + select[:, None, None] * w_grad[None], hid_grad

    starting = jnp.zeros((NE, FF, D), jnp.float32)
    expert_grad, hid_grads = lax.scan(per_slot, starting, (masked, hid_rows, weights, slot_experts))
    input_grad = hid_grads.reshape(slot_count * row_span, -1)
    new_momentum = momentum_decay * momentum + expert_grad
    new_master = master - learn_rate * new_momentum
    placed = new_master[next_experts[:, 0]].astype(jnp.bfloat16)
    return input_grad, new_momentum, new_master, placed
```

```python
import functools

import jax
import jax.numpy as jnp
from jax import lax
from jax.experimental import pallas as pl
from jax.experimental.pallas import tpu as pltpu
from jax.sharding import PartitionSpec as P

momentum_decay = 0.9
learn_rate = 0.01
BOTH = ("slot", "hid")
CHUNKS = ((0, 128),)
VM = pl.BlockSpec(memory_space=pltpu.VMEM)
SM = pl.BlockSpec(memory_space=pltpu.SMEM)
ANY = pl.BlockSpec(memory_space=pl.ANY)
MIB = 1 << 20


def params(mib):
    return pltpu.CompilerParams(vmem_limit_bytes=mib * MIB)


def cost(flops, moved):
    return pl.CostEstimate(flops=flops, bytes_accessed=moved, transcendentals=0)


def position(z, core, y, x):
    return (z * 2 + core) * 16 + y * 4 + x


def line_groups():
    groups = []
    for z in range(8):
        for line in range(4):
            groups.append([position(z, 0, line, k) for k in range(4)])
            groups.append([position(z, 1, k, line) for k in range(4)])
    return groups


def cross_pairs(step):
    pairs = []
    for z in range(8):
        for y in range(4):
            for x in range(4):
                pairs.append((position(z, 0, y, x), position(z, 0, (y + step) % 4, x)))
                pairs.append((position(z, 1, y, x), position(z, 1, y, (x + step) % 4)))
    return pairs


def mask_kernel(live_ref, cot_ref, *out_refs):
    rows = cot_ref.shape[0]
    live = lax.broadcasted_iota(jnp.int32, cot_ref.shape, 0) < live_ref[0]
    turned = jnp.where(live, cot_ref[...], jnp.zeros_like(cot_ref)).T
    for (start, size), out_ref in zip(CHUNKS, out_refs):
        for k in range(4):
            out_ref[k] = turned[start : start + size, :rows]


def masked_chunks(live, cotangent):
    rows = cotangent.shape[0]
    return pl.pallas_call(
        mask_kernel,
        out_shape=[jax.ShapeDtypeStruct((4, size, rows), jnp.bfloat16) for _, size in CHUNKS],
        in_specs=[SM, VM],
        out_specs=[VM] * len(CHUNKS),
        compiler_params=params(32),
        cost_estimate=cost(0, 3 * MIB),
        name="mask_turn",
    )(live, cotangent)


def block_of(place_ref, group, k):
    at = lax.rem(place_ref[1] + group, 4)
    return jnp.where(place_ref[0] == 0, 4 * at + k, 4 * k + at)


def slot_grad_kernel(layout, place_ref, hidden_ref, *refs):
    piece_refs, out_ref = refs[: len(layout)], refs[-1]
    for i, (group, first) in enumerate(layout):
        count, size, rows = piece_refs[i].shape
        grad = jnp.dot(
            piece_refs[i][...].reshape(count * size, rows),
            hidden_ref[...],
            preferred_element_type=jnp.float32,
        ).astype(jnp.bfloat16)
        for k in range(count):
            out_ref[block_of(place_ref, group, first + k)] = grad[k * size : (k + 1) * size]


def slot_grad(place, hidden, pieces, layout):
    size = pieces[0].shape[1]
    width = hidden.shape[1]
    return pl.pallas_call(
        functools.partial(slot_grad_kernel, layout),
        out_shape=jax.ShapeDtypeStruct((16, size, width), jnp.bfloat16),
        in_specs=[SM, VM] + [VM] * len(pieces),
        out_specs=VM,
        compiler_params=params(48),
        cost_estimate=cost(2 * 16 * size * width * hidden.shape[0], 12 * MIB),
        name="slot_grad",
    )(place, hidden, *pieces)


def update_kernel(now_ref, next_ref, got_ref, mom_ref, mas_ref, new_mom_ref, new_mas_ref, send_ref, rounded):
    experts = mom_ref.shape[0]
    size = mom_ref.shape[1]
    step = 32

    def rows_of(i, carry):
        at = pl.ds(pl.multiple_of(i * step, step), step)
        for e in range(experts):
            total = jnp.zeros((step, mom_ref.shape[2]), jnp.float32)
            for s in range(got_ref.shape[0]):
                held = (now_ref[s] == e).astype(jnp.float32)
                total += held * got_ref[s, at].astype(jnp.float32)
            new_mom = momentum_decay * mom_ref[e, at] + total
            new_mas = mas_ref[e, at] - learn_rate * new_mom
            new_mom_ref[e, at] = new_mom
            new_mas_ref[e, at] = new_mas
            rounded[e, at] = new_mas.astype(jnp.bfloat16)
        return carry

    lax.fori_loop(0, size // step, rows_of, 0)
    for s in range(send_ref.shape[0]):
        send_ref[s] = rounded[next_ref[s]]


def update(now, following, got, mom, mas):
    return pl.pallas_call(
        update_kernel,
        out_shape=[
            jax.ShapeDtypeStruct(mom.shape, jnp.float32),
            jax.ShapeDtypeStruct(mom.shape, jnp.float32),
            jax.ShapeDtypeStruct(got.shape, jnp.bfloat16),
        ],
        in_specs=[SM, SM, VM, VM, VM],
        out_specs=[VM] * 3,
        scratch_shapes=[pltpu.VMEM(mom.shape, jnp.bfloat16)],
        compiler_params=params(32),
        cost_estimate=cost(0, 8 * MIB),
        name="momentum_step",
    )(now, following, got, mom, mas)


def input_grad_kernel(layouts, place_ref, weight_ref, *refs):
    out_ref = refs[-1]
    total = None
    for group in range(4):
        rows_of_group, columns = [], []
        for k in range(4):
            for chunk_layout, base in layouts:
                for i, (at, first, count) in enumerate(chunk_layout):
                    if at == group and first <= k < first + count:
                        rows_of_group.append(refs[base + i][k - first])
            start = pl.multiple_of(block_of(place_ref, group, k) * 128, 128)
            columns.append(weight_ref[:, pl.ds(start, 128)])
        left = jnp.concatenate(rows_of_group, axis=0).T
        right = jnp.concatenate(columns, axis=1)
        part = lax.dot_general(
            left, right, (((1,), (1,)), ((), ())), preferred_element_type=jnp.float32
        )
        total = part if total is None else total + part
    out_ref[...] = total.astype(jnp.bfloat16)


def input_gradient(place, weights, chunk_pieces, layout):
    tile = 512
    width = weights.shape[0]
    rows = chunk_pieces[0][0].shape[2]
    flat, layouts = [], []
    for pieces in chunk_pieces:
        layouts.append(
            (tuple((g, f, p.shape[0]) for (g, f), p in zip(layout, pieces)), len(flat))
        )
        flat.extend(pieces)
    return pl.pallas_call(
        functools.partial(input_grad_kernel, layouts),
        grid=(rows // tile,),
        out_shape=jax.ShapeDtypeStruct((rows, width), jnp.bfloat16),
        in_specs=[SM, VM]
        + [pl.BlockSpec((p.shape[0], p.shape[1], tile), lambda i: (0, 0, i)) for p in flat],
        out_specs=pl.BlockSpec((tile, width), lambda i: (i, 0)),
        compiler_params=params(48),
        cost_estimate=cost(2 * rows * width * weights.shape[1], 12 * MIB),
        name="input_grad",
    )(place, weights, *flat)


def placed_kernel(*refs):
    out_ref = refs[-1]
    for j in range(16):
        block = jnp.concatenate([ref[j] for ref in refs[:-1]], axis=0)
        out_ref[:, j * 128 : (j + 1) * 128] = block.T


def place_weights(parts):
    width = parts[0].shape[2]
    return pl.pallas_call(
        placed_kernel,
        out_shape=jax.ShapeDtypeStruct((width, 2048), jnp.bfloat16),
        in_specs=[VM] * len(parts),
        out_specs=VM,
        compiler_params=params(32),
        cost_estimate=cost(0, 4 * MIB),
        name="placed_turn",
    )(*parts)


LAYOUT = ((0, 0), (3, 0), (3, 2), (1, 0), (1, 2), (2, 0), (2, 2))


def gather_hid(replicated):
    own = lax.all_to_all(
        replicated, BOTH, 0, 0, tiled=True, axis_index_groups=line_groups()
    )
    low, high = own[:2], own[2:]
    up, down = cross_pairs(1), cross_pairs(3)
    below_low = lax.ppermute(low, BOTH, up)
    above_high = lax.ppermute(high, BOTH, down)
    below_high = lax.ppermute(high, BOTH, up)
    above_low = lax.ppermute(low, BOTH, down)
    far_low = lax.ppermute(below_low, BOTH, up)
    far_high = lax.ppermute(above_high, BOTH, down)
    return (own, below_low, below_high, above_low, above_high, far_low, far_high)


def local(cotangent, hidden, weights, slot_experts, next_experts, row_counts, master, momentum):
    slot = lax.axis_index("slot")
    hid = lax.axis_index("hid")
    core = slot % 2
    place = jnp.stack([core, jnp.where(core == 0, hid // 4, hid % 4)]).astype(jnp.int32)
    live = lax.dynamic_slice_in_dim(row_counts, slot, 1)
    now, following = slot_experts[:, 0], next_experts[:, 0]
    mom = jnp.swapaxes(momentum, 1, 2)
    mas = jnp.swapaxes(master, 1, 2)

    new_mom, new_mas, parts, chunk_pieces = [], [], [], []
    for (start, size), replicated in zip(CHUNKS, masked_chunks(live, cotangent)):
        pieces = gather_hid(replicated)
        grads = slot_grad(place, hidden, pieces, LAYOUT)
        got = lax.all_to_all(grads, "slot", 0, 0, tiled=True)
        a, b, send = update(
            now, following, got, mom[:, start : start + size], mas[:, start : start + size]
        )
        parts.append(lax.all_to_all(send, "slot", 0, 0, tiled=True))
        new_mom.append(a)
        new_mas.append(b)
        chunk_pieces.append(pieces)

    input_grad = input_gradient(place, weights[0], chunk_pieces, LAYOUT)
    placed = place_weights(parts)[None]
    new_momentum = jnp.swapaxes(jnp.concatenate(new_mom, axis=1), 1, 2)
    new_master = jnp.swapaxes(jnp.concatenate(new_mas, axis=1), 1, 2)
    return (input_grad, new_momentum, new_master, placed)


def solution(mesh):
    return jax.shard_map(
        local,
        mesh=mesh,
        in_specs=(
            P("slot", "hid"),
            P("slot", "hid"),
            P("slot", "hid", None),
            P(),
            P(),
            P(),
            P(None, "hid", "slot"),
            P(None, "hid", "slot"),
        ),
        out_specs=(
            P("slot", "hid"),
            P(None, "hid", "slot"),
            P(None, "hid", "slot"),
            P("slot", "hid", None),
        ),
        check_vma=False,
    )
```

```python
import functools

import jax
import jax.numpy as jnp
from jax import lax
from jax.experimental import pallas as pl
from jax.experimental.pallas import tpu as pltpu
from jax.sharding import PartitionSpec as P

momentum_decay = 0.9
learn_rate = 0.01
BOTH = ("slot", "hid")
CHUNKS = ((0, 64), (64, 64))
VM = pl.BlockSpec(memory_space=pltpu.VMEM)
SM = pl.BlockSpec(memory_space=pltpu.SMEM)
HBM = pl.BlockSpec(memory_space=pltpu.HBM)
MIB = 1 << 20


def params(mib):
    return pltpu.CompilerParams(vmem_limit_bytes=mib * MIB)


def cost(flops, moved):
    return pl.CostEstimate(flops=flops, bytes_accessed=moved, transcendentals=0)


def position(z, core, y, x):
    return (z * 2 + core) * 16 + y * 4 + x


def line_pairs(step):
    pairs = []
    for z in range(8):
        for y in range(4):
            for x in range(4):
                pairs.append((position(z, 0, y, x), position(z, 0, y, (x + step) % 4)))
                pairs.append((position(z, 1, y, x), position(z, 1, (y + step) % 4, x)))
    return pairs


def cross_pairs(step):
    pairs = []
    for z in range(8):
        for y in range(4):
            for x in range(4):
                pairs.append((position(z, 0, y, x), position(z, 0, (y + step) % 4, x)))
                pairs.append((position(z, 1, y, x), position(z, 1, y, (x + step) % 4)))
    return pairs


def mask_kernel(place_ref, counts_ref, cot_ref, *out_refs):
    live = lax.broadcasted_iota(jnp.int32, cot_ref.shape, 0) < counts_ref[place_ref[3]]
    turned = jnp.where(live, cot_ref[...], jnp.zeros_like(cot_ref)).T
    for (start, size), out_ref in zip(CHUNKS, out_refs):
        out_ref[0] = turned[start : start + size]


def masked_chunks(place, counts, cotangent):
    rows = cotangent.shape[0]
    return pl.pallas_call(
        mask_kernel,
        out_shape=[jax.ShapeDtypeStruct((1, size, rows), jnp.bfloat16) for _, size in CHUNKS],
        in_specs=[SM, SM, VM],
        out_specs=[VM] * len(CHUNKS),
        compiler_params=params(16),
        cost_estimate=cost(0, 1 * MIB),
        name="mask_turn",
    )(place, counts, cotangent)


STEPS = ((0, 3), (1, 2))
NEAR = (0, 3, 1)
FAR = (2,)


def block_of(place_ref, group, k):
    cross = lax.rem(place_ref[1] + group, 4)
    line = lax.rem(place_ref[2] + k, 4)
    return jnp.where(place_ref[0] == 0, 4 * cross + line, 4 * line + cross)


def slot_grad_kernel(groups, place_ref, hidden_ref, *refs):
    piece_refs, (out_ref, stage, sems) = refs[: 2 * len(groups)], refs[-3:]
    copies = []
    for i, group in enumerate(groups):
        pair = piece_refs[2 * i : 2 * i + 2]
        _, size, rows = pair[0].shape
        grad = jnp.dot(
            jnp.concatenate([ref[...].reshape(2 * size, rows) for ref in pair], axis=0),
            hidden_ref[...],
            preferred_element_type=jnp.float32,
        ).astype(jnp.bfloat16)
        for at, k in enumerate(STEPS[0] + STEPS[1]):
            n = len(copies)
            stage[n] = grad[at * size : (at + 1) * size]
            copy = pltpu.make_async_copy(
                stage.at[n], out_ref.at[block_of(place_ref, group, k)], sems.at[n]
            )
            copy.start()
            copies.append(copy)
    for copy in copies:
        copy.wait()


def slot_grad(place, hidden, pieces, groups, into):
    size = pieces[0].shape[1]
    width = hidden.shape[1]
    blocks = 4 * len(groups)
    extra = () if into is None else (into,)
    return pl.pallas_call(
        functools.partial(slot_grad_kernel, groups),
        out_shape=jax.ShapeDtypeStruct((16, size, width), jnp.bfloat16),
        in_specs=[SM, VM] + [VM] * len(pieces) + [HBM] * len(extra),
        out_specs=HBM,
        input_output_aliases={2 + len(pieces): 0} if extra else {},
        scratch_shapes=[
            pltpu.VMEM((blocks, size, width), jnp.bfloat16),
            pltpu.SemaphoreType.DMA((blocks,)),
        ],
        compiler_params=params(32),
        cost_estimate=cost(2 * blocks * size * width * hidden.shape[0], 6 * MIB),
        name="slot_grad_far" if extra else "slot_grad_near",
    )(place, hidden, *pieces, *extra)


def expert_sum(now_ref, got_ref, e, at):
    total = jnp.zeros((at.size, got_ref.shape[2]), jnp.float32)
    for s in range(got_ref.shape[0]):
        total += (now_ref[s] == e).astype(jnp.float32) * got_ref[s, at].astype(jnp.float32)
    return total


def next_weights_kernel(wanted_only, now_ref, next_ref, got_ref, mom_ref, mas_ref, out_ref, rounded, sems):
    experts, size, _ = mom_ref.shape
    step = 16

    def rows_of(i, carry):
        at = pl.ds(pl.multiple_of(i * step, step), step)
        for e in range(experts):
            new_mom = momentum_decay * mom_ref[e, at] + expert_sum(now_ref, got_ref, e, at)
            rounded[e, at] = (mas_ref[e, at] - learn_rate * new_mom).astype(jnp.bfloat16)
        return carry

    lax.fori_loop(0, size // step, rows_of, 0)
    copies = []
    for s in range(out_ref.shape[0]):
        source = next_ref[s] if wanted_only else s
        copies.append(pltpu.make_async_copy(rounded.at[source], out_ref.at[s], sems.at[s]))
    for copy in copies:
        copy.start()
    for copy in copies:
        copy.wait()


def next_weights(wanted_only, now, following, got, mom, mas):
    count = got.shape[0] if wanted_only else mom.shape[0]
    return pl.pallas_call(
        functools.partial(next_weights_kernel, wanted_only),
        out_shape=jax.ShapeDtypeStruct((count,) + mom.shape[1:], jnp.bfloat16),
        in_specs=[SM, SM, VM, VM, VM],
        out_specs=HBM,
        scratch_shapes=[
            pltpu.VMEM(mom.shape, jnp.bfloat16),
            pltpu.SemaphoreType.DMA((count,)),
        ],
        compiler_params=params(16),
        cost_estimate=cost(0, 3 * MIB),
        name="next_weights",
    )(now, following, got, mom, mas)


def update_kernel(now_ref, mom_ref, mas_ref, *refs):
    got_refs, (new_mom_ref, new_mas_ref, total) = refs[:-3], refs[-3:]
    e = pl.program_id(0)
    start = 0
    for got_ref in got_refs:
        for first in range(0, got_ref.shape[1], 16):
            total[start + first : start + first + 16] = expert_sum(
                now_ref, got_ref, e, pl.ds(first, 16)
            )
        start += got_ref.shape[1]
    new_mom = momentum_decay * mom_ref[0] + total[...].T
    new_mom_ref[0] = new_mom
    new_mas_ref[0] = mas_ref[0] - learn_rate * new_mom


def update(now, momentum, master, gots):
    experts, width, columns = momentum.shape
    block = pl.BlockSpec((1, width, columns), lambda e: (e, 0, 0))
    return pl.pallas_call(
        update_kernel,
        grid=(experts,),
        out_shape=[jax.ShapeDtypeStruct(momentum.shape, jnp.float32)] * 2,
        in_specs=[SM, block, block]
        + [pl.BlockSpec(g.shape, lambda e: (0, 0, 0)) for g in gots],
        out_specs=[block, block],
        scratch_shapes=[pltpu.VMEM((columns, width), jnp.float32)],
        compiler_params=params(24),
        cost_estimate=cost(0, 8 * MIB),
        name="momentum_step",
    )(now, momentum, master, *gots)


def input_grad_kernel(place_ref, weight_ref, *refs):
    pieces, out_ref = refs[:-1], refs[-1]
    total = None
    for i, group in enumerate(NEAR + FAR):
        rows_of_group, columns = [], []
        for half, steps in enumerate(STEPS):
            for n, k in enumerate(steps):
                for chunk in range(len(CHUNKS)):
                    rows_of_group.append(pieces[8 * chunk + 2 * i + half][n])
                start = pl.multiple_of(block_of(place_ref, group, k) * 128, 128)
                columns.append(weight_ref[:, pl.ds(start, 128)])
        left = jnp.concatenate(rows_of_group, axis=0).T
        right = jnp.concatenate(columns, axis=1)
        part = lax.dot_general(
            left, right, (((1,), (1,)), ((), ())), preferred_element_type=jnp.float32
        )
        total = part if total is None else total + part
    out_ref[...] = total.astype(jnp.bfloat16)


def input_gradient(place, weights, pieces):
    tile = 512
    width = weights.shape[0]
    rows = pieces[0].shape[2]
    return pl.pallas_call(
        input_grad_kernel,
        grid=(rows // tile,),
        out_shape=jax.ShapeDtypeStruct((rows, width), jnp.bfloat16),
        in_specs=[SM, VM]
        + [pl.BlockSpec((p.shape[0], p.shape[1], tile), lambda i: (0, 0, i)) for p in pieces],
        out_specs=pl.BlockSpec((tile, width), lambda i: (i, 0)),
        compiler_params=params(32),
        cost_estimate=cost(2 * rows * width * weights.shape[1], 12 * MIB),
        name="input_grad",
    )(place, weights, *pieces)


def placed_kernel(wanted_ref, all_ref, own_ref, out_ref):
    for j in range(2):
        block = jnp.concatenate([all_ref[j, 0], own_ref[j]], axis=0)
        out_ref[:, j * 128 : (j + 1) * 128] = block.T


def place_weights(wanted, every, own):
    slots, size, width = own.shape
    return pl.pallas_call(
        placed_kernel,
        grid_spec=pltpu.PrefetchScalarGridSpec(
            num_scalar_prefetch=1,
            grid=(slots // 2,),
            in_specs=[
                pl.BlockSpec((2, 1) + every.shape[2:], lambda i, wanted: (i, wanted[0], 0, 0)),
                pl.BlockSpec((2, size, width), lambda i, wanted: (i, 0, 0)),
            ],
            out_specs=pl.BlockSpec((width, 256), lambda i, wanted: (0, i)),
        ),
        out_shape=jax.ShapeDtypeStruct((width, slots * 128), jnp.bfloat16),
        compiler_params=params(16),
        cost_estimate=cost(0, 4 * MIB),
        name="placed_turn",
    )(wanted, every, own)


def gather_line(own):
    back = lax.ppermute(own, BOTH, line_pairs(1))
    ahead = lax.ppermute(own, BOTH, line_pairs(3))
    across = lax.ppermute(own, BOTH, line_pairs(2))
    return jnp.concatenate([own, back], axis=0), jnp.concatenate([ahead, across], axis=0)


def gather_cross(one, two):
    up, down = cross_pairs(1), cross_pairs(3)
    one_below = lax.ppermute(one, BOTH, up)
    one_above = lax.ppermute(one, BOTH, down)
    two_below = lax.ppermute(two, BOTH, up)
    two_above = lax.ppermute(two, BOTH, down)
    one_far = lax.ppermute(one_below, BOTH, up)
    two_far = lax.ppermute(two_above, BOTH, down)
    return (one, two, one_below, two_below, one_above, two_above, one_far, two_far)


def local(cotangent, hidden, weights, slot_experts, next_experts, row_counts, master, momentum):
    slot = lax.axis_index("slot")
    hid = lax.axis_index("hid")
    core = slot & 1
    y, x = hid >> 2, hid & 3
    place = jnp.stack(
        [core, jnp.where(core == 0, y, x), jnp.where(core == 0, x, y), slot]
    ).astype(jnp.int32)
    now, following = slot_experts[:, 0], next_experts[:, 0]

    first, second = masked_chunks(place, row_counts, cotangent)
    first_one, first_two = gather_line(first)
    second, first_one = lax.optimization_barrier((second, first_one))
    first_pieces = gather_cross(first_one, first_two)
    second_pieces = gather_cross(*gather_line(second))

    hidden, mom, mas = lax.optimization_barrier(
        (hidden, jnp.swapaxes(momentum, 1, 2), jnp.swapaxes(master, 1, 2))
    )
    def grads_of(pieces):
        near = slot_grad(place, hidden, pieces[:6], NEAR, None)
        return slot_grad(place, hidden, pieces[6:], FAR, near)

    got_first = lax.all_to_all(grads_of(first_pieces), "slot", 0, 0, tiled=True)
    got_first, second_grads = lax.optimization_barrier((got_first, grads_of(second_pieces)))
    gots = (got_first, lax.all_to_all(second_grads, "slot", 0, 0, tiled=True))
    (cut, size), (rest, _) = CHUNKS
    every = next_weights(False, now, following, gots[0], mom[:, cut : cut + size], mas[:, cut : cut + size])
    every = lax.all_gather(every, "slot", axis=0)
    wanted = next_weights(True, now, following, gots[1], mom[:, rest:], mas[:, rest:])
    wanted = lax.all_to_all(wanted, "slot", 0, 0, tiled=True)

    new_momentum, new_master = update(now, momentum, master, gots)
    input_grad = input_gradient(place, weights[0], first_pieces + second_pieces)
    placed = place_weights(lax.dynamic_slice_in_dim(following, slot, 1), every, wanted)[None]
    return (input_grad, new_momentum, new_master, placed)


def solution(mesh):
    return jax.shard_map(
        local,
        mesh=mesh,
        in_specs=(
            P("slot", "hid"),
            P("slot", "hid"),
            P("slot", "hid", None),
            P(),
            P(),
            P(),
            P(None, "hid", "slot"),
            P(None, "hid", "slot"),
        ),
        out_specs=(
            P("slot", "hid"),
            P(None, "hid", "slot"),
            P(None, "hid", "slot"),
            P("slot", "hid", None),
        ),
        check_vma=False,
    )
```

```python
import functools

import jax
import jax.numpy as jnp
from jax import lax
from jax.experimental import pallas as pl
from jax.experimental.pallas import tpu as pltpu
from jax.sharding import PartitionSpec as P

momentum_decay = 0.9
learn_rate = 0.01
BOTH = ("slot", "hid")
VM = pl.BlockSpec(memory_space=pltpu.VMEM)
SM = pl.BlockSpec(memory_space=pltpu.SMEM)
HBM = pl.BlockSpec(memory_space=pltpu.HBM)
MIB = 1 << 20


def params(mib):
    return pltpu.CompilerParams(vmem_limit_bytes=mib * MIB)


def cost(flops, moved):
    return pl.CostEstimate(flops=flops, bytes_accessed=moved, transcendentals=0)


def position(z, core, y, x):
    return (z * 2 + core) * 16 + y * 4 + x


def line_pairs(step):
    pairs = []
    for z in range(8):
        for y in range(4):
            for x in range(4):
                pairs.append((position(z, 0, y, x), position(z, 0, y, (x + step) % 4)))
                pairs.append((position(z, 1, y, x), position(z, 1, (y + step) % 4, x)))
    return pairs


def cross_pairs(step):
    pairs = []
    for z in range(8):
        for y in range(4):
            for x in range(4):
                pairs.append((position(z, 0, y, x), position(z, 0, (y + step) % 4, x)))
                pairs.append((position(z, 1, y, x), position(z, 1, y, (x + step) % 4)))
    return pairs


def mask_kernel(place_ref, counts_ref, cot_ref, out_ref):
    live = lax.broadcasted_iota(jnp.int32, cot_ref.shape, 0) < counts_ref[place_ref[3]]
    out_ref[...] = jnp.where(live, cot_ref[...], jnp.zeros_like(cot_ref)).T


def masked_block(place, counts, cotangent):
    return pl.pallas_call(
        mask_kernel,
        out_shape=jax.ShapeDtypeStruct(cotangent.shape[::-1], jnp.bfloat16),
        in_specs=[SM, SM, VM],
        out_specs=VM,
        compiler_params=params(16),
        cost_estimate=cost(0, 1 * MIB),
        name="mask_turn",
    )(place, counts, cotangent)


STEPS = (0, 3, 1, 2)
GROUPS = (0, 3, 1, 2)


def block_of(place_ref, group, k):
    cross = lax.rem(place_ref[1] + group, 4)
    line = lax.rem(place_ref[2] + k, 4)
    return jnp.where(place_ref[0] == 0, 4 * cross + line, 4 * line + cross)


def fetch(refs, held, sems):
    copies = [
        pltpu.make_async_copy(ref, held.at[n], sems.at[n]) for n, ref in enumerate(refs)
    ]
    for copy in copies:
        copy.start()
    return copies


def slot_grad_kernel(groups, place_ref, hidden_ref, *refs):
    piece_refs, (out_ref, held, stage, in_sems, sems) = refs[: 4 * len(groups)], refs[-5:]
    loads = fetch(piece_refs, held, in_sems)
    copies = []
    _, size, rows = held.shape
    for i, group in enumerate(groups):
        for load in loads[4 * i : 4 * i + 4]:
            load.wait()
        grad = jnp.dot(
            held[4 * i : 4 * i + 4].reshape(4 * size, rows),
            hidden_ref[...],
            preferred_element_type=jnp.float32,
        ).astype(jnp.bfloat16)
        for at, k in enumerate(STEPS):
            n = len(copies)
            stage[n] = grad[at * size : (at + 1) * size]
            copy = pltpu.make_async_copy(
                stage.at[n], out_ref.at[block_of(place_ref, group, k)], sems.at[n]
            )
            copy.start()
            copies.append(copy)
    for copy in copies:
        copy.wait()


def slot_grad(place, hidden, pieces, groups, into):
    size, rows = pieces[0].shape
    width = hidden.shape[1]
    extra = () if into is None else (into,)
    return pl.pallas_call(
        functools.partial(slot_grad_kernel, groups),
        out_shape=jax.ShapeDtypeStruct((16, size, width), jnp.bfloat16),
        in_specs=[SM, VM] + [HBM] * (len(pieces) + len(extra)),
        out_specs=HBM,
        input_output_aliases={2 + len(pieces): 0} if extra else {},
        scratch_shapes=[
            pltpu.VMEM((len(pieces), size, rows), jnp.bfloat16),
            pltpu.VMEM((len(pieces), size, width), jnp.bfloat16),
            pltpu.SemaphoreType.DMA((len(pieces),)),
            pltpu.SemaphoreType.DMA((len(pieces),)),
        ],
        compiler_params=params(32),
        cost_estimate=cost(2 * len(pieces) * size * width * rows, 6 * MIB),
        name="slot_grad",
    )(place, hidden, *pieces, *extra)


def expert_sum(now_ref, got_ref, e, at):
    total = None
    for s in range(got_ref.shape[0]):
        part = (now_ref[s] == e).astype(jnp.float32) * got_ref[s, at].astype(jnp.float32)
        total = part if total is None else total + part
    return total


def next_weights_kernel(now_ref, next_ref, got_ref, base_ref, out_ref, rounded):
    experts, size, _ = base_ref.shape
    step = 32

    def rows_of(i, carry):
        at = pl.ds(pl.multiple_of(i * step, step), step)
        for e in range(experts):
            total = expert_sum(now_ref, got_ref, e, at)
            rounded[e, at] = (base_ref[e, at] - learn_rate * total).astype(jnp.bfloat16)
        return carry

    lax.fori_loop(0, size // step, rows_of, 0)
    for s in range(out_ref.shape[0]):
        out_ref[s] = rounded[next_ref[s]]


def next_weights(now, following, got, base):
    return pl.pallas_call(
        next_weights_kernel,
        out_shape=jax.ShapeDtypeStruct(got.shape, jnp.bfloat16),
        in_specs=[SM, SM, VM, VM],
        out_specs=VM,
        scratch_shapes=[pltpu.VMEM(base.shape, jnp.bfloat16)],
        compiler_params=params(16),
        cost_estimate=cost(0, 6 * MIB),
        name="next_weights",
    )(now, following, got, base)


def update_kernel(now_ref, mom_ref, mas_ref, got_ref, new_mom_ref, new_mas_ref, total):
    e = pl.program_id(0)
    for first in range(0, total.shape[0], 16):
        total[first : first + 16] = expert_sum(now_ref, got_ref, e, pl.ds(first, 16))
    new_mom = momentum_decay * mom_ref[0] + total[...].T
    new_mom_ref[0] = new_mom
    new_mas_ref[0] = mas_ref[0] - learn_rate * new_mom


def update(now, momentum, master, got):
    experts, width, columns = momentum.shape
    block = pl.BlockSpec((1, width, columns), lambda e: (e, 0, 0))
    return pl.pallas_call(
        update_kernel,
        grid=(experts,),
        out_shape=[jax.ShapeDtypeStruct(momentum.shape, jnp.float32)] * 2,
        in_specs=[SM, block, block, pl.BlockSpec(got.shape, lambda e: (0, 0, 0))],
        out_specs=[block, block],
        scratch_shapes=[pltpu.VMEM((columns, width), jnp.float32)],
        compiler_params=params(24),
        cost_estimate=cost(0, 8 * MIB),
        name="momentum_step",
    )(now, momentum, master, got)


def input_grad_kernel(place_ref, weight_ref, *refs):
    piece_refs, (out_ref, held, sems) = refs[:-3], refs[-3:]
    tile = out_ref.shape[0]
    tiles = held.shape[-1] // tile
    now = pl.program_id(0)

    def load(n, t):
        part = pl.ds(t * tile, tile)
        return pltpu.make_async_copy(
            piece_refs[n].at[:, part], held.at[n, :, part], sems.at[t, n]
        )

    @pl.when(now == 0)
    def _():
        for t in range(tiles):
            for n in range(len(piece_refs)):
                load(n, t).start()

    here = pl.multiple_of(now * tile, tile)
    for n in range(len(piece_refs)):
        part = pl.ds(here, tile)
        pltpu.make_async_copy(
            piece_refs[n].at[:, part], held.at[n, :, part], sems.at[now, n]
        ).wait()
    total = None
    for i, group in enumerate(GROUPS):
        rows_of_group, columns = [], []
        for n, k in enumerate(STEPS):
            rows_of_group.append(held[4 * i + n, :, pl.ds(here, tile)])
            start = pl.multiple_of(block_of(place_ref, group, k) * 128, 128)
            columns.append(weight_ref[:, pl.ds(start, 128)])
        left = jnp.concatenate(rows_of_group, axis=0).T
        right = jnp.concatenate(columns, axis=1)
        part = lax.dot_general(
            left, right, (((1,), (1,)), ((), ())), preferred_element_type=jnp.float32
        )
        total = part if total is None else total + part
    out_ref[...] = total.astype(jnp.bfloat16)


def input_gradient(place, weights, pieces):
    tile = 512
    width = weights.shape[0]
    rows = pieces[0].shape[1]
    return pl.pallas_call(
        input_grad_kernel,
        grid=(rows // tile,),
        out_shape=jax.ShapeDtypeStruct((rows, width), jnp.bfloat16),
        in_specs=[SM, VM] + [HBM] * len(pieces),
        out_specs=pl.BlockSpec((tile, width), lambda i: (i, 0)),
        scratch_shapes=[
            pltpu.VMEM((len(pieces),) + pieces[0].shape, jnp.bfloat16),
            pltpu.SemaphoreType.DMA((rows // tile, len(pieces))),
        ],
        compiler_params=params(32),
        cost_estimate=cost(2 * rows * width * weights.shape[1], 12 * MIB),
        name="input_grad",
    )(place, weights, *pieces)


def placed_kernel(got_ref, out_ref):
    for j in range(got_ref.shape[0]):
        out_ref[:, j * 128 : (j + 1) * 128] = got_ref[j].T


def place_weights(got):
    slots, size, width = got.shape
    return pl.pallas_call(
        placed_kernel,
        out_shape=jax.ShapeDtypeStruct((width, slots * size), jnp.bfloat16),
        in_specs=[VM],
        out_specs=VM,
        compiler_params=params(16),
        cost_estimate=cost(0, 4 * MIB),
        name="placed_turn",
    )(got)


def gather_hid(own):
    on, back, up, down = line_pairs(1), line_pairs(3), cross_pairs(1), cross_pairs(3)
    behind = lax.ppermute(own, BOTH, on)
    ahead = lax.ppermute(own, BOTH, back)
    below = [lax.ppermute(own, BOTH, up)]
    above = [lax.ppermute(own, BOTH, down)]
    across = lax.ppermute(behind, BOTH, on)
    line = [own, behind, ahead, across]
    below += [lax.ppermute(p, BOTH, up) for p in line[1:]]
    above += [lax.ppermute(p, BOTH, down) for p in line[1:]]
    far = [lax.ppermute(p, BOTH, up) for p in below[:2]]
    far += [lax.ppermute(p, BOTH, down) for p in above[2:]]
    return line, below, above, far


def local(cotangent, hidden, weights, slot_experts, next_experts, row_counts, master, momentum):
    slot = lax.axis_index("slot")
    hid = lax.axis_index("hid")
    core = slot & 1
    y, x = hid >> 2, hid & 3
    place = jnp.stack(
        [core, jnp.where(core == 0, y, x), jnp.where(core == 0, x, y), slot]
    ).astype(jnp.int32)
    now, following = slot_experts[:, 0], next_experts[:, 0]

    line, below, above, far = gather_hid(masked_block(place, row_counts, cotangent))
    grads = slot_grad(place, hidden, line, GROUPS[:1], None)
    grads = slot_grad(place, hidden, below + above, GROUPS[1:3], grads)
    grads = slot_grad(place, hidden, far, GROUPS[3:], grads)
    got = lax.all_to_all(grads, "slot", 0, 0, tiled=True)
    input_grad = input_gradient(place, weights[0], line + below + above + far)
    got, input_grad = lax.optimization_barrier((got, input_grad))
    base = jnp.swapaxes(master - (learn_rate * momentum_decay) * momentum, 1, 2)
    arrived = lax.all_to_all(next_weights(now, following, got, base), "slot", 0, 0, tiled=True)

    new_momentum, new_master = update(now, momentum, master, got)
    placed = place_weights(arrived)[None]
    return (input_grad, new_momentum, new_master, placed)


def solution(mesh):
    return jax.shard_map(
        local,
        mesh=mesh,
        in_specs=(
            P("slot", "hid"),
            P("slot", "hid"),
            P("slot", "hid", None),
            P(),
            P(),
            P(),
            P(None, "hid", "slot"),
            P(None, "hid", "slot"),
        ),
        out_specs=(
            P("slot", "hid"),
            P(None, "hid", "slot"),
            P(None, "hid", "slot"),
            P("slot", "hid", None),
        ),
        check_vma=False,
    )
```

```python
import functools

import jax
import jax.numpy as jnp
from jax import lax
from jax.experimental import pallas as pl
from jax.experimental.pallas import tpu as pltpu
from jax.sharding import PartitionSpec as P

momentum_decay = 0.9
learn_rate = 0.01
BOTH = ("slot", "hid")
VM = pl.BlockSpec(memory_space=pltpu.VMEM)
SM = pl.BlockSpec(memory_space=pltpu.SMEM)
HBM = pl.BlockSpec(memory_space=pltpu.HBM)
MIB = 1 << 20


def params(mib):
    return pltpu.CompilerParams(vmem_limit_bytes=mib * MIB)


def cost(flops, moved):
    return pl.CostEstimate(flops=flops, bytes_accessed=moved, transcendentals=0)


def position(z, core, y, x):
    return (z * 2 + core) * 16 + y * 4 + x


def line_pairs(step):
    pairs = []
    for z in range(8):
        for y in range(4):
            for x in range(4):
                pairs.append((position(z, 0, y, x), position(z, 0, y, (x + step) % 4)))
                pairs.append((position(z, 1, y, x), position(z, 1, (y + step) % 4, x)))
    return pairs


def cross_pairs(step):
    pairs = []
    for z in range(8):
        for y in range(4):
            for x in range(4):
                pairs.append((position(z, 0, y, x), position(z, 0, (y + step) % 4, x)))
                pairs.append((position(z, 1, y, x), position(z, 1, y, (x + step) % 4)))
    return pairs


def mask_kernel(place_ref, counts_ref, cot_ref, out_ref):
    live = lax.broadcasted_iota(jnp.int32, cot_ref.shape, 0) < counts_ref[place_ref[3]]
    out_ref[...] = jnp.where(live, cot_ref[...], jnp.zeros_like(cot_ref)).T


def masked_block(place, counts, cotangent):
    return pl.pallas_call(
        mask_kernel,
        out_shape=jax.ShapeDtypeStruct(cotangent.shape[::-1], jnp.bfloat16),
        in_specs=[SM, SM, VM],
        out_specs=VM,
        compiler_params=params(16),
        cost_estimate=cost(0, 1 * MIB),
        name="mask_turn",
    )(place, counts, cotangent)


STEPS = (0, 3, 1, 2)
GROUPS = (0, 3, 1, 2)


def block_of(place_ref, group, k):
    cross = lax.rem(place_ref[1] + group, 4)
    line = lax.rem(place_ref[2] + k, 4)
    return jnp.where(place_ref[0] == 0, 4 * cross + line, 4 * line + cross)


def fetch(refs, held, sems):
    copies = [
        pltpu.make_async_copy(ref, held.at[n], sems.at[n]) for n, ref in enumerate(refs)
    ]
    for copy in copies:
        copy.start()
    return copies


def slot_grad_kernel(groups, keep, place_ref, hidden_ref, *refs):
    piece_refs = refs[: 4 * len(groups)]
    held, stage, in_sems, sems, keep_sems = refs[-5:]
    out_ref = refs[-7] if keep else refs[-6]
    loads = fetch(piece_refs, held, in_sems)
    copies, kept = [], []
    _, size, rows = held.shape
    for i, group in enumerate(groups):
        for n in range(4 * i, 4 * i + 4):
            loads[n].wait()
            if keep:
                kept.append(pltpu.make_async_copy(held.at[n], refs[-6].at[n], keep_sems.at[n]))
                kept[n].start()
        grad = jnp.dot(
            held[4 * i : 4 * i + 4].reshape(4 * size, rows),
            hidden_ref[...],
            preferred_element_type=jnp.float32,
        ).astype(jnp.bfloat16)
        for at, k in enumerate(STEPS):
            n = len(copies)
            stage[n] = grad[at * size : (at + 1) * size]
            copy = pltpu.make_async_copy(
                stage.at[n], out_ref.at[block_of(place_ref, group, k)], sems.at[n]
            )
            copy.start()
            copies.append(copy)
    for copy in copies + kept:
        copy.wait()


def slot_grad(place, hidden, pieces, groups, into, keep=False):
    size, rows = pieces[0].shape
    width = hidden.shape[1]
    extra = () if into is None else (into,)
    shapes = [jax.ShapeDtypeStruct((16, size, width), jnp.bfloat16)]
    if keep:
        shapes.append(jax.ShapeDtypeStruct((len(pieces), size, rows), jnp.bfloat16))
    return pl.pallas_call(
        functools.partial(slot_grad_kernel, groups, keep),
        out_shape=shapes,
        in_specs=[SM, VM] + [HBM] * (len(pieces) + len(extra)),
        out_specs=[HBM] * len(shapes),
        input_output_aliases={2 + len(pieces): 0} if extra else {},
        scratch_shapes=[
            pltpu.VMEM((len(pieces), size, rows), jnp.bfloat16),
            pltpu.VMEM((len(pieces), size, width), jnp.bfloat16),
            pltpu.SemaphoreType.DMA((len(pieces),)),
            pltpu.SemaphoreType.DMA((len(pieces),)),
            pltpu.SemaphoreType.DMA((len(pieces),)),
        ],
        compiler_params=params(32),
        cost_estimate=cost(2 * len(pieces) * size * width * rows, 6 * MIB),
        name="slot_grad",
    )(place, hidden, *pieces, *extra)


def expert_sum(now_ref, got_ref, e, at):
    total = None
    for s in range(got_ref.shape[0]):
        part = (now_ref[s] == e).astype(jnp.float32) * got_ref[s, at].astype(jnp.float32)
        total = part if total is None else total + part
    return total


def next_weights_kernel(now_ref, next_ref, got_ref, base_ref, out_ref, rounded):
    experts, size, _ = base_ref.shape
    step = 32

    def rows_of(i, carry):
        at = pl.ds(pl.multiple_of(i * step, step), step)
        for e in range(experts):
            total = expert_sum(now_ref, got_ref, e, at)
            rounded[e, at] = (base_ref[e, at] - learn_rate * total).astype(jnp.bfloat16)
        return carry

    lax.fori_loop(0, size // step, rows_of, 0)
    for s in range(out_ref.shape[0]):
        out_ref[s] = rounded[next_ref[s]]


def next_weights(now, following, got, base):
    return pl.pallas_call(
        next_weights_kernel,
        out_shape=jax.ShapeDtypeStruct(got.shape, jnp.bfloat16),
        in_specs=[SM, SM, VM, VM],
        out_specs=VM,
        scratch_shapes=[pltpu.VMEM(base.shape, jnp.bfloat16)],
        compiler_params=params(16),
        cost_estimate=cost(0, 6 * MIB),
        name="next_weights",
    )(now, following, got, base)


def update_kernel(now_ref, mom_ref, mas_ref, got_ref, new_mom_ref, new_mas_ref, total):
    e = pl.program_id(0)
    for first in range(0, total.shape[0], 16):
        total[first : first + 16] = expert_sum(now_ref, got_ref, e, pl.ds(first, 16))
    new_mom = momentum_decay * mom_ref[0] + total[...].T
    new_mom_ref[0] = new_mom
    new_mas_ref[0] = mas_ref[0] - learn_rate * new_mom


def update(now, momentum, master, got):
    experts, width, columns = momentum.shape
    block = pl.BlockSpec((1, width, columns), lambda e: (e, 0, 0))
    return pl.pallas_call(
        update_kernel,
        grid=(experts,),
        out_shape=[jax.ShapeDtypeStruct(momentum.shape, jnp.float32)] * 2,
        in_specs=[SM, block, block, pl.BlockSpec(got.shape, lambda e: (0, 0, 0))],
        out_specs=[block, block],
        scratch_shapes=[pltpu.VMEM((columns, width), jnp.float32)],
        compiler_params=params(24),
        cost_estimate=cost(0, 8 * MIB),
        name="momentum_step",
    )(now, momentum, master, got)


def input_grad_kernel(place_ref, weight_ref, *refs):
    piece_refs, (far_ref, out_ref, held, sems) = refs[:-4], refs[-4:]
    piece_refs += tuple(far_ref.at[n] for n in range(4))
    tile = out_ref.shape[0]
    tiles = held.shape[-1] // tile
    now = pl.program_id(0)

    def load(n, t):
        part = pl.ds(t * tile, tile)
        return pltpu.make_async_copy(
            piece_refs[n].at[:, part], held.at[n, :, part], sems.at[t, n]
        )

    @pl.when(now == 0)
    def _():
        for t in range(tiles):
            for n in range(len(piece_refs)):
                load(n, t).start()

    here = pl.multiple_of(now * tile, tile)
    for n in range(len(piece_refs)):
        part = pl.ds(here, tile)
        pltpu.make_async_copy(
            piece_refs[n].at[:, part], held.at[n, :, part], sems.at[now, n]
        ).wait()
    total = None
    for i, group in enumerate(GROUPS):
        rows_of_group, columns = [], []
        for n, k in enumerate(STEPS):
            rows_of_group.append(held[4 * i + n, :, pl.ds(here, tile)])
            start = pl.multiple_of(block_of(place_ref, group, k) * 128, 128)
            columns.append(weight_ref[:, pl.ds(start, 128)])
        left = jnp.concatenate(rows_of_group, axis=0).T
        right = jnp.concatenate(columns, axis=1)
        part = lax.dot_general(
            left, right, (((1,), (1,)), ((), ())), preferred_element_type=jnp.float32
        )
        total = part if total is None else total + part
    out_ref[...] = total.astype(jnp.bfloat16)


def input_gradient(place, weights, pieces, far):
    tile = 512
    width = weights.shape[0]
    rows = pieces[0].shape[1]
    return pl.pallas_call(
        input_grad_kernel,
        grid=(rows // tile,),
        out_shape=jax.ShapeDtypeStruct((rows, width), jnp.bfloat16),
        in_specs=[SM, VM] + [HBM] * (len(pieces) + 1),
        out_specs=pl.BlockSpec((tile, width), lambda i: (i, 0)),
        scratch_shapes=[
            pltpu.VMEM((16,) + pieces[0].shape, jnp.bfloat16),
            pltpu.SemaphoreType.DMA((rows // tile, 16)),
        ],
        compiler_params=params(32),
        cost_estimate=cost(2 * rows * width * weights.shape[1], 12 * MIB),
        name="input_grad",
    )(place, weights, *pieces, far)


def placed_kernel(got_ref, out_ref, held, turned, in_sems, sems):
    slots = got_ref.shape[0]
    loads = fetch([got_ref.at[j] for j in range(slots)], held, in_sems)
    copies = []
    for j in range(slots):
        loads[j].wait()
        turned[j] = held[j].T
        columns = pl.ds(j * 128, 128)
        copies.append(pltpu.make_async_copy(turned.at[j], out_ref.at[:, columns], sems.at[j]))
        copies[j].start()
    for copy in copies:
        copy.wait()


def place_weights(got):
    slots, size, width = got.shape
    return pl.pallas_call(
        placed_kernel,
        out_shape=jax.ShapeDtypeStruct((width, slots * size), jnp.bfloat16),
        in_specs=[HBM],
        out_specs=HBM,
        scratch_shapes=[
            pltpu.VMEM(got.shape, jnp.bfloat16),
            pltpu.VMEM((slots, width, size), jnp.bfloat16),
            pltpu.SemaphoreType.DMA((slots,)),
            pltpu.SemaphoreType.DMA((slots,)),
        ],
        compiler_params=params(16),
        cost_estimate=cost(0, 4 * MIB),
        name="placed_turn",
    )(got)


def gather_hid(own):
    on, back, up, down = line_pairs(1), line_pairs(3), cross_pairs(1), cross_pairs(3)
    behind = lax.ppermute(own, BOTH, on)
    ahead = lax.ppermute(own, BOTH, back)
    below = [lax.ppermute(own, BOTH, up)]
    above = [lax.ppermute(own, BOTH, down)]
    across = lax.ppermute(behind, BOTH, on)
    line = [own, behind, ahead, across]
    below += [lax.ppermute(p, BOTH, up) for p in line[1:]]
    above += [lax.ppermute(p, BOTH, down) for p in line[1:]]
    far = [lax.ppermute(p, BOTH, up) for p in below[:2]]
    far += [lax.ppermute(p, BOTH, down) for p in above[2:]]
    return line, below, above, far


def local(cotangent, hidden, weights, slot_experts, next_experts, row_counts, master, momentum):
    slot = lax.axis_index("slot")
    hid = lax.axis_index("hid")
    core = slot & 1
    y, x = hid >> 2, hid & 3
    place = jnp.stack(
        [core, jnp.where(core == 0, y, x), jnp.where(core == 0, x, y), slot]
    ).astype(jnp.int32)
    now, following = slot_experts[:, 0], next_experts[:, 0]

    line, below, above, far = gather_hid(masked_block(place, row_counts, cotangent))
    (grads,) = slot_grad(place, hidden, line, GROUPS[:1], None)
    (grads,) = slot_grad(place, hidden, below + above, GROUPS[1:3], grads)
    grads, far = slot_grad(place, hidden, far, GROUPS[3:], grads, keep=True)
    got = lax.all_to_all(grads, "slot", 0, 0, tiled=True)
    input_grad = input_gradient(place, weights[0], line + below + above, far)
    old_master, old_momentum, input_grad = lax.optimization_barrier((master, momentum, input_grad))
    base = jnp.swapaxes(old_master - (learn_rate * momentum_decay) * old_momentum, 1, 2)
    arrived = lax.all_to_all(next_weights(now, following, got, base), "slot", 0, 0, tiled=True)

    new_momentum, new_master = update(now, momentum, master, got)
    placed = place_weights(arrived)[None]
    return (input_grad, new_momentum, new_master, placed)


def solution(mesh):
    return jax.shard_map(
        local,
        mesh=mesh,
        in_specs=(
            P("slot", "hid"),
            P("slot", "hid"),
            P("slot", "hid", None),
            P(),
            P(),
            P(),
            P(None, "hid", "slot"),
            P(None, "hid", "slot"),
        ),
        out_specs=(
            P("slot", "hid"),
            P(None, "hid", "slot"),
            P(None, "hid", "slot"),
            P("slot", "hid", None),
        ),
        check_vma=False,
    )
```

```python
import functools

import jax
import jax.numpy as jnp
from jax import lax
from jax.experimental import pallas as pl
from jax.experimental.pallas import tpu as pltpu
from jax.sharding import PartitionSpec as P

momentum_decay = 0.9
learn_rate = 0.01
BOTH = ("slot", "hid")
VM = pl.BlockSpec(memory_space=pltpu.VMEM)
SM = pl.BlockSpec(memory_space=pltpu.SMEM)
HBM = pl.BlockSpec(memory_space=pltpu.HBM)
MIB = 1 << 20


def params(mib):
    return pltpu.CompilerParams(vmem_limit_bytes=mib * MIB)


def cost(flops, moved):
    return pl.CostEstimate(flops=flops, bytes_accessed=moved, transcendentals=0)


def position(z, core, y, x):
    return (z * 2 + core) * 16 + y * 4 + x


def line_pairs(step):
    pairs = []
    for z in range(8):
        for y in range(4):
            for x in range(4):
                pairs.append((position(z, 0, y, x), position(z, 0, y, (x + step) % 4)))
                pairs.append((position(z, 1, y, x), position(z, 1, (y + step) % 4, x)))
    return pairs


def cross_pairs(step):
    pairs = []
    for z in range(8):
        for y in range(4):
            for x in range(4):
                pairs.append((position(z, 0, y, x), position(z, 0, (y + step) % 4, x)))
                pairs.append((position(z, 1, y, x), position(z, 1, y, (x + step) % 4)))
    return pairs


def mask_kernel(place_ref, counts_ref, cot_ref, out_ref):
    live = lax.broadcasted_iota(jnp.int32, cot_ref.shape, 0) < counts_ref[place_ref[3]]
    out_ref[...] = jnp.where(live, cot_ref[...], jnp.zeros_like(cot_ref)).T


def masked_block(place, counts, cotangent):
    return pl.pallas_call(
        mask_kernel,
        out_shape=jax.ShapeDtypeStruct(cotangent.shape[::-1], jnp.bfloat16),
        in_specs=[SM, SM, VM],
        out_specs=VM,
        compiler_params=params(16),
        cost_estimate=cost(0, 1 * MIB),
        name="mask_turn",
    )(place, counts, cotangent)


STEPS = (0, 3, 1, 2)
GROUPS = (0, 3, 1, 2)


def block_of(place_ref, group, k):
    cross = lax.rem(place_ref[1] + group, 4)
    line = lax.rem(place_ref[2] + k, 4)
    return jnp.where(place_ref[0] == 0, 4 * cross + line, 4 * line + cross)


def fetch(refs, held, sems):
    copies = [
        pltpu.make_async_copy(ref, held.at[n], sems.at[n]) for n, ref in enumerate(refs)
    ]
    for copy in copies:
        copy.start()
    return copies


def slot_grad_kernel(groups, keep, place_ref, hidden_ref, *refs):
    count = 4 * len(groups)
    piece_refs = refs[:count]
    second_half = ()
    if keep:
        second_half, piece_refs = refs[2:3], refs[:2] + refs[3 : count + 1]
    held, stage, in_sems, sems, keep_sems = refs[-5:]
    out_ref = refs[-7] if keep else refs[-6]
    _, size, rows = held.shape
    loads, copies, kept = [], [], []
    for n, ref in enumerate(piece_refs):
        loads.append(
            pltpu.make_async_copy(ref, held.at[n, pl.ds(0, ref.shape[0])], in_sems.at[n])
        )
    for ref in second_half:
        half = ref.shape[0]
        loads.append(
            pltpu.make_async_copy(ref, held.at[1, pl.ds(size - half, half)], in_sems.at[count])
        )
    for load in loads:
        load.start()
    for load in loads[count:]:
        load.wait()
    for i, group in enumerate(groups):
        for n in range(4 * i, 4 * i + 4):
            loads[n].wait()
            if keep:
                kept.append(pltpu.make_async_copy(held.at[n], refs[-6].at[n], keep_sems.at[n]))
                kept[n].start()
        grad = jnp.dot(
            held[4 * i : 4 * i + 4].reshape(4 * size, rows),
            hidden_ref[...],
            preferred_element_type=jnp.float32,
        ).astype(jnp.bfloat16)
        for at, k in enumerate(STEPS):
            n = len(copies)
            stage[n] = grad[at * size : (at + 1) * size]
            copy = pltpu.make_async_copy(
                stage.at[n], out_ref.at[block_of(place_ref, group, k)], sems.at[n]
            )
            copy.start()
            copies.append(copy)
    for copy in copies + kept:
        copy.wait()


def slot_grad(place, hidden, pieces, groups, into, keep=False):
    size, rows = pieces[0].shape
    width = hidden.shape[1]
    blocks = 4 * len(groups)
    extra = () if into is None else (into,)
    shapes = [jax.ShapeDtypeStruct((16, size, width), jnp.bfloat16)]
    if keep:
        shapes.append(jax.ShapeDtypeStruct((blocks, size, rows), jnp.bfloat16))
    return pl.pallas_call(
        functools.partial(slot_grad_kernel, groups, keep),
        out_shape=shapes,
        in_specs=[SM, VM] + [HBM] * (len(pieces) + len(extra)),
        out_specs=[HBM] * len(shapes),
        input_output_aliases={2 + len(pieces): 0} if extra else {},
        scratch_shapes=[
            pltpu.VMEM((blocks, size, rows), jnp.bfloat16),
            pltpu.VMEM((blocks, size, width), jnp.bfloat16),
            pltpu.SemaphoreType.DMA((len(pieces),)),
            pltpu.SemaphoreType.DMA((len(pieces),)),
            pltpu.SemaphoreType.DMA((len(pieces),)),
        ],
        compiler_params=params(32),
        cost_estimate=cost(2 * len(pieces) * size * width * rows, 6 * MIB),
        name="slot_grad",
    )(place, hidden, *pieces, *extra)


def expert_sum(now_ref, got_ref, e, at):
    total = None
    for s in range(got_ref.shape[0]):
        part = (now_ref[s] == e).astype(jnp.float32) * got_ref[s, at].astype(jnp.float32)
        total = part if total is None else total + part
    return total


def next_weights_kernel(now_ref, next_ref, got_ref, base_ref, out_ref, rounded):
    experts, size, _ = base_ref.shape
    step = 32

    def rows_of(i, carry):
        at = pl.ds(pl.multiple_of(i * step, step), step)
        for e in range(experts):
            total = expert_sum(now_ref, got_ref, e, at)
            rounded[e, at] = (base_ref[e, at] - learn_rate * total).astype(jnp.bfloat16)
        return carry

    lax.fori_loop(0, size // step, rows_of, 0)
    for s in range(out_ref.shape[0]):
        out_ref[s] = rounded[next_ref[s]]


def next_weights(now, following, got, base):
    return pl.pallas_call(
        next_weights_kernel,
        out_shape=jax.ShapeDtypeStruct(got.shape, jnp.bfloat16),
        in_specs=[SM, SM, VM, VM],
        out_specs=VM,
        scratch_shapes=[pltpu.VMEM(base.shape, jnp.bfloat16)],
        compiler_params=params(16),
        cost_estimate=cost(0, 6 * MIB),
        name="next_weights",
    )(now, following, got, base)


def update_kernel(now_ref, mom_ref, mas_ref, got_ref, new_mom_ref, new_mas_ref, total):
    e = pl.program_id(0)
    for first in range(0, total.shape[0], 16):
        total[first : first + 16] = expert_sum(now_ref, got_ref, e, pl.ds(first, 16))
    new_mom = momentum_decay * mom_ref[0] + total[...].T
    new_mom_ref[0] = new_mom
    new_mas_ref[0] = mas_ref[0] - learn_rate * new_mom


def update(now, momentum, master, got):
    experts, width, columns = momentum.shape
    block = pl.BlockSpec((1, width, columns), lambda e: (e, 0, 0))
    return pl.pallas_call(
        update_kernel,
        grid=(experts,),
        out_shape=[jax.ShapeDtypeStruct(momentum.shape, jnp.float32)] * 2,
        in_specs=[SM, block, block, pl.BlockSpec(got.shape, lambda e: (0, 0, 0))],
        out_specs=[block, block],
        scratch_shapes=[pltpu.VMEM((columns, width), jnp.float32)],
        compiler_params=params(24),
        cost_estimate=cost(0, 8 * MIB),
        name="momentum_step",
    )(now, momentum, master, got)


def input_grad_kernel(place_ref, weight_ref, *refs):
    piece_refs, (far_ref, out_ref, held, sems) = refs[:-4], refs[-4:]
    piece_refs += tuple(far_ref.at[n] for n in range(4))
    tile = out_ref.shape[0]
    tiles = held.shape[-1] // tile
    now = pl.program_id(0)

    def load(n, t):
        part = pl.ds(t * tile, tile)
        return pltpu.make_async_copy(
            piece_refs[n].at[:, part], held.at[n, :, part], sems.at[t, n]
        )

    @pl.when(now == 0)
    def _():
        for t in range(tiles):
            for n in range(len(piece_refs)):
                load(n, t).start()

    here = pl.multiple_of(now * tile, tile)
    for n in range(len(piece_refs)):
        part = pl.ds(here, tile)
        pltpu.make_async_copy(
            piece_refs[n].at[:, part], held.at[n, :, part], sems.at[now, n]
        ).wait()
    total = None
    for i, group in enumerate(GROUPS):
        rows_of_group, columns = [], []
        for n, k in enumerate(STEPS):
            rows_of_group.append(held[4 * i + n, :, pl.ds(here, tile)])
            start = pl.multiple_of(block_of(place_ref, group, k) * 128, 128)
            columns.append(weight_ref[:, pl.ds(start, 128)])
        left = jnp.concatenate(rows_of_group, axis=0).T
        right = jnp.concatenate(columns, axis=1)
        part = lax.dot_general(
            left, right, (((1,), (1,)), ((), ())), preferred_element_type=jnp.float32
        )
        total = part if total is None else total + part
    out_ref[...] = total.astype(jnp.bfloat16)


def input_gradient(place, weights, pieces, far):
    tile = 512
    width = weights.shape[0]
    rows = pieces[0].shape[1]
    return pl.pallas_call(
        input_grad_kernel,
        grid=(rows // tile,),
        out_shape=jax.ShapeDtypeStruct((rows, width), jnp.bfloat16),
        in_specs=[SM, VM] + [HBM] * (len(pieces) + 1),
        out_specs=pl.BlockSpec((tile, width), lambda i: (i, 0)),
        scratch_shapes=[
            pltpu.VMEM((16,) + pieces[0].shape, jnp.bfloat16),
            pltpu.SemaphoreType.DMA((rows // tile, 16)),
        ],
        compiler_params=params(32),
        cost_estimate=cost(2 * rows * width * weights.shape[1], 12 * MIB),
        name="input_grad",
    )(place, weights, *pieces, far)


def placed_kernel(got_ref, out_ref, held, turned, in_sems, sems):
    slots = got_ref.shape[0]
    loads = fetch([got_ref.at[j] for j in range(slots)], held, in_sems)
    copies = []
    for j in range(slots):
        loads[j].wait()
        turned[j] = held[j].T
        columns = pl.ds(j * 128, 128)
        copies.append(pltpu.make_async_copy(turned.at[j], out_ref.at[:, columns], sems.at[j]))
        copies[j].start()
    for copy in copies:
        copy.wait()


def place_weights(got):
    slots, size, width = got.shape
    return pl.pallas_call(
        placed_kernel,
        out_shape=jax.ShapeDtypeStruct((width, slots * size), jnp.bfloat16),
        in_specs=[HBM],
        out_specs=HBM,
        scratch_shapes=[
            pltpu.VMEM(got.shape, jnp.bfloat16),
            pltpu.VMEM((slots, width, size), jnp.bfloat16),
            pltpu.SemaphoreType.DMA((slots,)),
            pltpu.SemaphoreType.DMA((slots,)),
        ],
        compiler_params=params(16),
        cost_estimate=cost(0, 4 * MIB),
        name="placed_turn",
    )(got)


def gather_hid(own):
    on, back, up, down = line_pairs(1), line_pairs(3), cross_pairs(1), cross_pairs(3)
    behind = lax.ppermute(own, BOTH, on)
    ahead = lax.ppermute(own, BOTH, back)
    below = [lax.ppermute(own, BOTH, up)]
    above = [lax.ppermute(own, BOTH, down)]
    across = lax.ppermute(behind, BOTH, on)
    line = [own, behind, ahead, across]
    below += [lax.ppermute(p, BOTH, up) for p in line[1:]]
    above += [lax.ppermute(p, BOTH, down) for p in line[1:]]
    half = own.shape[0] // 2
    far = [lax.ppermute(below[0], BOTH, up), lax.ppermute(below[1][:half], BOTH, up)]
    far += [lax.ppermute(p, BOTH, down) for p in (above[1][half:], above[2], above[3])]
    return line, below, above, far


def local(cotangent, hidden, weights, slot_experts, next_experts, row_counts, master, momentum):
    slot = lax.axis_index("slot")
    hid = lax.axis_index("hid")
    core = slot & 1
    y, x = hid >> 2, hid & 3
    place = jnp.stack(
        [core, jnp.where(core == 0, y, x), jnp.where(core == 0, x, y), slot]
    ).astype(jnp.int32)
    now, following = slot_experts[:, 0], next_experts[:, 0]

    line, below, above, far = gather_hid(masked_block(place, row_counts, cotangent))
    (grads,) = slot_grad(place, hidden, line, GROUPS[:1], None)
    (grads,) = slot_grad(place, hidden, below + above, GROUPS[1:3], grads)
    grads, far = slot_grad(place, hidden, far, GROUPS[3:], grads, keep=True)
    got = lax.all_to_all(grads, "slot", 0, 0, tiled=True)
    input_grad = input_gradient(place, weights[0], line + below + above, far)
    old_master, old_momentum, input_grad = lax.optimization_barrier((master, momentum, input_grad))
    base = jnp.swapaxes(old_master - (learn_rate * momentum_decay) * old_momentum, 1, 2)
    arrived = lax.all_to_all(next_weights(now, following, got, base), "slot", 0, 0, tiled=True)

    new_momentum, new_master = update(now, momentum, master, got)
    placed = place_weights(arrived)[None]
    return (input_grad, new_momentum, new_master, placed)


def solution(mesh):
    return jax.shard_map(
        local,
        mesh=mesh,
        in_specs=(
            P("slot", "hid"),
            P("slot", "hid"),
            P("slot", "hid", None),
            P(),
            P(),
            P(),
            P(None, "hid", "slot"),
            P(None, "hid", "slot"),
        ),
        out_specs=(
            P("slot", "hid"),
            P(None, "hid", "slot"),
            P(None, "hid", "slot"),
            P("slot", "hid", None),
        ),
        check_vma=False,
    )
```

```python
import functools

import jax
import jax.numpy as jnp
from jax import lax
from jax.experimental import pallas as pl
from jax.experimental.pallas import tpu as pltpu
from jax.sharding import PartitionSpec as P

momentum_decay = 0.9
learn_rate = 0.01
BOTH = ("slot", "hid")
VM = pl.BlockSpec(memory_space=pltpu.VMEM)
SM = pl.BlockSpec(memory_space=pltpu.SMEM)
HBM = pl.BlockSpec(memory_space=pltpu.HBM)
MIB = 1 << 20


def params(mib):
    return pltpu.CompilerParams(vmem_limit_bytes=mib * MIB)


def cost(flops, moved):
    return pl.CostEstimate(flops=flops, bytes_accessed=moved, transcendentals=0)


def position(z, core, y, x):
    return (z * 2 + core) * 16 + y * 4 + x


def line_pairs(step):
    pairs = []
    for z in range(8):
        for y in range(4):
            for x in range(4):
                pairs.append((position(z, 0, y, x), position(z, 0, y, (x + step) % 4)))
                pairs.append((position(z, 1, y, x), position(z, 1, (y + step) % 4, x)))
    return pairs


def cross_pairs(step):
    pairs = []
    for z in range(8):
        for y in range(4):
            for x in range(4):
                pairs.append((position(z, 0, y, x), position(z, 0, (y + step) % 4, x)))
                pairs.append((position(z, 1, y, x), position(z, 1, y, (x + step) % 4)))
    return pairs


def mask_kernel(place_ref, counts_ref, cot_ref, out_ref, held, sems):
    parts, step, _ = held.shape
    loads = fetch([cot_ref.at[pl.ds(n * step, step)] for n in range(parts)], held, sems)
    for n in range(parts):
        loads[n].wait()
        rows = held[n]
        live = lax.broadcasted_iota(jnp.int32, rows.shape, 0) + n * step < counts_ref[place_ref[3]]
        out_ref[:, n * step : (n + 1) * step] = jnp.where(live, rows, jnp.zeros_like(rows)).T


def masked_block(place, counts, cotangent):
    rows, columns = cotangent.shape
    parts = 4
    return pl.pallas_call(
        mask_kernel,
        out_shape=jax.ShapeDtypeStruct((columns, rows), jnp.bfloat16),
        in_specs=[SM, SM, HBM],
        out_specs=VM,
        scratch_shapes=[
            pltpu.VMEM((parts, rows // parts, columns), jnp.bfloat16),
            pltpu.SemaphoreType.DMA((parts,)),
        ],
        compiler_params=params(16),
        cost_estimate=cost(0, 1 * MIB),
        name="mask_turn",
    )(place, counts, cotangent)


STEPS = (0, 3, 1, 2)
GROUPS = (0, 3, 1, 2)


def block_of(place_ref, group, k):
    cross = lax.rem(place_ref[1] + group, 4)
    line = lax.rem(place_ref[2] + k, 4)
    return jnp.where(place_ref[0] == 0, 4 * cross + line, 4 * line + cross)


def fetch(refs, held, sems):
    copies = [
        pltpu.make_async_copy(ref, held.at[n], sems.at[n]) for n, ref in enumerate(refs)
    ]
    for copy in copies:
        copy.start()
    return copies


def slot_grad_kernel(groups, keep, place_ref, hidden_ref, *refs):
    count = 4 * len(groups)
    piece_refs = refs[:count]
    second_half = ()
    if keep:
        second_half, piece_refs = refs[2:3], refs[:2] + refs[3 : count + 1]
    held, stage, in_sems, sems, keep_sems = refs[-5:]
    out_ref = refs[-7] if keep else refs[-6]
    _, size, rows = held.shape
    loads, copies, kept = [], [], []
    for n, ref in enumerate(piece_refs):
        loads.append(
            pltpu.make_async_copy(ref, held.at[n, pl.ds(0, ref.shape[0])], in_sems.at[n])
        )
    for ref in second_half:
        half = ref.shape[0]
        loads.append(
            pltpu.make_async_copy(ref, held.at[1, pl.ds(size - half, half)], in_sems.at[count])
        )
    for load in loads:
        load.start()
    for load in loads[count:]:
        load.wait()
    for i, group in enumerate(groups):
        for n in range(4 * i, 4 * i + 4):
            loads[n].wait()
            if keep:
                kept.append(pltpu.make_async_copy(held.at[n], refs[-6].at[n], keep_sems.at[n]))
                kept[n].start()
        grad = jnp.dot(
            held[4 * i : 4 * i + 4].reshape(4 * size, rows),
            hidden_ref[...],
            preferred_element_type=jnp.float32,
        ).astype(jnp.bfloat16)
        for at, k in enumerate(STEPS):
            n = len(copies)
            stage[n] = grad[at * size : (at + 1) * size]
            copy = pltpu.make_async_copy(
                stage.at[n], out_ref.at[block_of(place_ref, group, k)], sems.at[n]
            )
            copy.start()
            copies.append(copy)
    for copy in copies + kept:
        copy.wait()


def slot_grad(place, hidden, pieces, groups, into, keep=False):
    size, rows = pieces[0].shape
    width = hidden.shape[1]
    blocks = 4 * len(groups)
    extra = () if into is None else (into,)
    shapes = [jax.ShapeDtypeStruct((16, size, width), jnp.bfloat16)]
    if keep:
        shapes.append(jax.ShapeDtypeStruct((blocks, size, rows), jnp.bfloat16))
    return pl.pallas_call(
        functools.partial(slot_grad_kernel, groups, keep),
        out_shape=shapes,
        in_specs=[SM, VM] + [HBM] * (len(pieces) + len(extra)),
        out_specs=[HBM] * len(shapes),
        input_output_aliases={2 + len(pieces): 0} if extra else {},
        scratch_shapes=[
            pltpu.VMEM((blocks, size, rows), jnp.bfloat16),
            pltpu.VMEM((blocks, size, width), jnp.bfloat16),
            pltpu.SemaphoreType.DMA((len(pieces),)),
            pltpu.SemaphoreType.DMA((len(pieces),)),
            pltpu.SemaphoreType.DMA((len(pieces),)),
        ],
        compiler_params=params(32),
        cost_estimate=cost(2 * len(pieces) * size * width * rows, 6 * MIB),
        name="slot_grad",
    )(place, hidden, *pieces, *extra)


def expert_sum(now_ref, got_ref, e, at):
    total = None
    for s in range(got_ref.shape[0]):
        part = (now_ref[s] == e).astype(jnp.float32) * got_ref[s, at].astype(jnp.float32)
        total = part if total is None else total + part
    return total


def next_weights_kernel(now_ref, next_ref, got_ref, base_ref, out_ref, rounded):
    experts, size, _ = base_ref.shape
    step = 32

    def rows_of(i, carry):
        at = pl.ds(pl.multiple_of(i * step, step), step)
        for e in range(experts):
            total = expert_sum(now_ref, got_ref, e, at)
            rounded[e, at] = (base_ref[e, at] - learn_rate * total).astype(jnp.bfloat16)
        return carry

    lax.fori_loop(0, size // step, rows_of, 0)
    for s in range(out_ref.shape[0]):
        out_ref[s] = rounded[next_ref[s]]


def next_weights(now, following, got, base):
    return pl.pallas_call(
        next_weights_kernel,
        out_shape=jax.ShapeDtypeStruct(got.shape, jnp.bfloat16),
        in_specs=[SM, SM, VM, VM],
        out_specs=VM,
        scratch_shapes=[pltpu.VMEM(base.shape, jnp.bfloat16)],
        compiler_params=params(16),
        cost_estimate=cost(0, 6 * MIB),
        name="next_weights",
    )(now, following, got, base)


def update_kernel(now_ref, mom_ref, mas_ref, got_ref, new_mom_ref, new_mas_ref, total):
    e = pl.program_id(0)
    for first in range(0, total.shape[0], 16):
        total[first : first + 16] = expert_sum(now_ref, got_ref, e, pl.ds(first, 16))
    new_mom = momentum_decay * mom_ref[0] + total[...].T
    new_mom_ref[0] = new_mom
    new_mas_ref[0] = mas_ref[0] - learn_rate * new_mom


def update(now, momentum, master, got):
    experts, width, columns = momentum.shape
    block = pl.BlockSpec((1, width, columns), lambda e: (e, 0, 0))
    return pl.pallas_call(
        update_kernel,
        grid=(experts,),
        out_shape=[jax.ShapeDtypeStruct(momentum.shape, jnp.float32)] * 2,
        in_specs=[SM, block, block, pl.BlockSpec(got.shape, lambda e: (0, 0, 0))],
        out_specs=[block, block],
        scratch_shapes=[pltpu.VMEM((columns, width), jnp.float32)],
        compiler_params=params(24),
        cost_estimate=cost(0, 8 * MIB),
        name="momentum_step",
    )(now, momentum, master, got)


def input_grad_kernel(place_ref, weight_ref, *refs):
    piece_refs, (far_ref, out_ref, held, sems) = refs[:-4], refs[-4:]
    piece_refs += tuple(far_ref.at[n] for n in range(4))
    tile = out_ref.shape[0]
    tiles = held.shape[-1] // tile
    now = pl.program_id(0)

    def load(n, t):
        part = pl.ds(t * tile, tile)
        return pltpu.make_async_copy(
            piece_refs[n].at[:, part], held.at[n, :, part], sems.at[t, n]
        )

    @pl.when(now == 0)
    def _():
        for t in range(tiles):
            for n in range(len(piece_refs)):
                load(n, t).start()

    here = pl.multiple_of(now * tile, tile)
    for n in range(len(piece_refs)):
        part = pl.ds(here, tile)
        pltpu.make_async_copy(
            piece_refs[n].at[:, part], held.at[n, :, part], sems.at[now, n]
        ).wait()
    total = None
    for i, group in enumerate(GROUPS):
        rows_of_group, columns = [], []
        for n, k in enumerate(STEPS):
            rows_of_group.append(held[4 * i + n, :, pl.ds(here, tile)])
            start = pl.multiple_of(block_of(place_ref, group, k) * 128, 128)
            columns.append(weight_ref[:, pl.ds(start, 128)])
        left = jnp.concatenate(rows_of_group, axis=0).T
        right = jnp.concatenate(columns, axis=1)
        part = lax.dot_general(
            left, right, (((1,), (1,)), ((), ())), preferred_element_type=jnp.float32
        )
        total = part if total is None else total + part
    out_ref[...] = total.astype(jnp.bfloat16)


def input_gradient(place, weights, pieces, far):
    tile = 512
    width = weights.shape[0]
    rows = pieces[0].shape[1]
    return pl.pallas_call(
        input_grad_kernel,
        grid=(rows // tile,),
        out_shape=jax.ShapeDtypeStruct((rows, width), jnp.bfloat16),
        in_specs=[SM, VM] + [HBM] * (len(pieces) + 1),
        out_specs=pl.BlockSpec((tile, width), lambda i: (i, 0)),
        scratch_shapes=[
            pltpu.VMEM((16,) + pieces[0].shape, jnp.bfloat16),
            pltpu.SemaphoreType.DMA((rows // tile, 16)),
        ],
        compiler_params=params(32),
        cost_estimate=cost(2 * rows * width * weights.shape[1], 12 * MIB),
        name="input_grad",
    )(place, weights, *pieces, far)


def placed_kernel(got_ref, out_ref, held, turned, in_sems, sems):
    slots = got_ref.shape[0]
    loads = fetch([got_ref.at[j] for j in range(slots)], held, in_sems)
    copies = []
    for j in range(slots):
        loads[j].wait()
        turned[j] = held[j].T
        columns = pl.ds(j * 128, 128)
        copies.append(pltpu.make_async_copy(turned.at[j], out_ref.at[:, columns], sems.at[j]))
        copies[j].start()
    for copy in copies:
        copy.wait()


def place_weights(got):
    slots, size, width = got.shape
    return pl.pallas_call(
        placed_kernel,
        out_shape=jax.ShapeDtypeStruct((width, slots * size), jnp.bfloat16),
        in_specs=[HBM],
        out_specs=HBM,
        scratch_shapes=[
            pltpu.VMEM(got.shape, jnp.bfloat16),
            pltpu.VMEM((slots, width, size), jnp.bfloat16),
            pltpu.SemaphoreType.DMA((slots,)),
            pltpu.SemaphoreType.DMA((slots,)),
        ],
        compiler_params=params(16),
        cost_estimate=cost(0, 4 * MIB),
        name="placed_turn",
    )(got)


def gather_hid(own):
    on, back, up, down = line_pairs(1), line_pairs(3), cross_pairs(1), cross_pairs(3)
    behind = lax.ppermute(own, BOTH, on)
    ahead = lax.ppermute(own, BOTH, back)
    below = [lax.ppermute(own, BOTH, up)]
    above = [lax.ppermute(own, BOTH, down)]
    across = lax.ppermute(behind, BOTH, on)
    line = [own, behind, ahead, across]
    below += [lax.ppermute(p, BOTH, up) for p in line[1:]]
    above += [lax.ppermute(p, BOTH, down) for p in line[1:]]
    half = own.shape[0] // 2
    far = [lax.ppermute(below[0], BOTH, up), lax.ppermute(below[1][:half], BOTH, up)]
    far += [lax.ppermute(p, BOTH, down) for p in (above[1][half:], above[2], above[3])]
    return line, below, above, far


def local(cotangent, hidden, weights, slot_experts, next_experts, row_counts, master, momentum):
    slot = lax.axis_index("slot")
    hid = lax.axis_index("hid")
    core = slot & 1
    y, x = hid >> 2, hid & 3
    place = jnp.stack(
        [core, jnp.where(core == 0, y, x), jnp.where(core == 0, x, y), slot]
    ).astype(jnp.int32)
    now, following = slot_experts[:, 0], next_experts[:, 0]

    line, below, above, far = gather_hid(masked_block(place, row_counts, cotangent))
    (grads,) = slot_grad(place, hidden, line, GROUPS[:1], None)
    (grads,) = slot_grad(place, hidden, below + above, GROUPS[1:3], grads)
    grads, far = slot_grad(place, hidden, far, GROUPS[3:], grads, keep=True)
    got = lax.all_to_all(grads, "slot", 0, 0, tiled=True)
    input_grad = input_gradient(place, weights[0], line + below + above, far)
    old_master, old_momentum, input_grad = lax.optimization_barrier((master, momentum, input_grad))
    base = jnp.swapaxes(old_master - (learn_rate * momentum_decay) * old_momentum, 1, 2)
    arrived = lax.all_to_all(next_weights(now, following, got, base), "slot", 0, 0, tiled=True)

    new_momentum, new_master = update(now, momentum, master, got)
    placed = place_weights(arrived)[None]
    return (input_grad, new_momentum, new_master, placed)


def solution(mesh):
    return jax.shard_map(
        local,
        mesh=mesh,
        in_specs=(
            P("slot", "hid"),
            P("slot", "hid"),
            P("slot", "hid", None),
            P(),
            P(),
            P(),
            P(None, "hid", "slot"),
            P(None, "hid", "slot"),
        ),
        out_specs=(
            P("slot", "hid"),
            P(None, "hid", "slot"),
            P(None, "hid", "slot"),
            P("slot", "hid", None),
        ),
        check_vma=False,
    )
```
